32 devices in a mesh: rep: 2 (over y), tp: 4 (over z), ad: 4 (over x, core).
Axes of the slice: x: 2, y: 2, z: 4, core: 2. Of those that a mesh axis runs over, the one named last changes fastest.
Arguments:
- tokens: bfloat16 [6144, 8192], P(('rep', 'ad'), 'tp'), parts along dimension 0
- query_base_weight: bfloat16 [8192, 512], P('ad', 'tp'), may hold values from -0.0625 to 0.0625
- adapter_down_weight: bfloat16 [128, 8192, 64], P('ad', 'tp'), may hold values from -0.0625 to 0.0625
- adapter_up_weight: bfloat16 [128, 64, 512], P('ad', None, 'tp'), may hold values from -0.75 to 0.75
- rotated_key_cache: bfloat16 [6144, 4, 128], P(('rep', 'ad')), parts along dimension 0
- value_cache_rows: bfloat16 [6144, 4, 128], P(('rep', 'ad')), parts along dimension 0, may hold values from -6 to 6
- segment_index: int32 [8, 768], P(('rep', 'ad')), parts along dimension 0, may hold values from 0 to 7, never falling along the last dimension, each value on 1 to 256 neighbouring positions
- tenant_index: int32 [8, 8], P(('rep', 'ad')), parts along dimension 0, may hold values from 0 to 127, as said below
Outputs:
- attention: bfloat16 [6144, 512], P(('rep', 'ad'), 'tp'), parts along dimension 0
The draws below stay inside these ranges and needn't reach their ends.
There are 2 independent parts, one for each index of `rep`. The reference program is written for one: setup_inputs(seed, part) draws one part's arguments, and reference() takes and returns one part's arrays. A program takes and returns all parts, laid end to end along the dimension named above; an argument that names none is the same for every part. Nothing has to cross between parts.
Inputs may be any that keep to these rules, and one draw needn't show every extreme that they name: `tenant_index`: adapter a is held by owner a // 32 along ad, in its slot a mod 32. Among the 8 sequences of one batch at most 4 use adapters of one owner, and one owner is used by exactly 4 sequences of every batch. `segment_index`: within a batch segment numbers never fall; sequence s is the tokens numbered s, each has 1 to 256 tokens and one has exactly 256.
All inputs are finite; a program needn't handle non-finite values.
Results may differ from the reference program's by a relative error of at most 0.012.
The reference program's roundings to bfloat16 on the way (of `shrink_b`, `queries` and `probs`) count: a program that leaves them out, or rounds other values in their place, can miss the bound.
Values may be sent and summed in bfloat16 or wider, within the bound.
A program may use at most 192 MiB of HBM per device.

```python
import math
import jax
import jax.numpy as jnp
import numpy as np
from jax import lax

MODEL_WIDTH = 8192
HD = 128
ADAPTER_RANK = 64
TOK_DEV = 768
SEQUENCE_COUNT = 8
CAP = 4
ADAPT_DEV = 32
HEADS = 4
KVH = 4
QUERY_WIDTH = 512
MOST = 256
BATCHES = 4
ADAPTER_COUNT = 128
TOKENS = 3072


def draw_tokens(key, part):
    key = jax.random.fold_in(key, 5)
    key_data = jax.random.fold_in(key, 0)
    result = jnp.clip(jax.random.normal(key_data, (TOKENS, MODEL_WIDTH), jnp.float32), -6.0, 6.0)
    return result.astype(jnp.bfloat16)


def draw_rotated_key_cache(key, part):
    key = jax.random.fold_in(key, 7)
    key_data = jax.random.fold_in(key, 0)
    result = jnp.clip(jax.random.normal(key_data, (TOKENS, KVH, HD), jnp.float32), -6.0, 6.0)
    return result.astype(jnp.bfloat16)


def draw_tenant_index(key, part):
    key = jax.random.fold_in(key, 11)
    key_main, key_other, key_order, key_slot, key_tilt = jax.random.split(key, 5)
    favored = jax.random.randint(key_main, (), 0, BATCHES)
    others = (favored + 1 + jax.random.randint(key_other, (BATCHES, SEQUENCE_COUNT - CAP), 0, BATCHES - 1)) % BATCHES
    owners = jnp.concatenate([jnp.full((BATCHES, CAP), favored, jnp.int32), others.astype(jnp.int32)], axis=1)
    scores = jax.random.randint(key_order, (BATCHES, SEQUENCE_COUNT), 0, 1 << 20) * SEQUENCE_COUNT + jnp.arange(SEQUENCE_COUNT, dtype=jnp.int32)[None, :]
    ordering = jnp.argsort(scores, axis=1, stable=True)
    owners = jnp.take_along_axis(owners, ordering, axis=1)
    slot_base = jax.random.randint(key_slot, (BATCHES, SEQUENCE_COUNT), 0, ADAPT_DEV)
    slot_tilt = jax.random.randint(key_tilt, (BATCHES, SEQUENCE_COUNT), 1, ADAPT_DEV + 1)
    slots = slot_base * slot_tilt // ADAPT_DEV
    return (owners * ADAPT_DEV + slots).astype(jnp.int32)


def levels(own_key, extent, shards, least, largest):
    gain, own = 1.0, jax.random.fold_in(own_key, 6)
    for axis_at, parts in shards:
        steps = jnp.exp(jax.random.uniform(jax.random.fold_in(own, axis_at), (parts,), jnp.float32, least / len(shards), largest / len(shards)))
        gain = gain * jnp.repeat(steps, extent[axis_at] // parts).reshape([-1 if axis == axis_at else 1 for axis in range(len(extent))])
    return gain


def length_profile(count, total, bound, lean):
    loads = [(1 << 20) // math.isqrt(grade ** lean) + 1 for grade in range(2, count + 1)]
    spare, given = total - bound - (count - 1), [1] * (count - 1)
    while spare > 0:
        candidates = [i for i in range(count - 1) if given[i] < bound]
        whole, left = sum([loads[i] for i in candidates]), spare
        for i in candidates:
            extra = min(bound - given[i], max(1, left * loads[i] // whole), spare)
            given[i] = given[i] + extra
            spare = spare - extra
    return np.array([bound] + given)


def uneven_parts(key, amount, total, reach, skew):
    if amount == 2:
        one = jax.random.randint(key, (), max(1, total - reach), min(reach, total - 1) + 1)
        return jnp.stack([one, total - one])
    tallies = jnp.asarray(length_profile(amount, total, reach, skew), jnp.int32)
    pairs = (amount - 1) // 2
    giver, sink = tallies[1:1 + 2 * pairs:2], tallies[2:2 + 2 * pairs:2]
    room = jnp.minimum(giver - 1, reach - sink)
    passed = jax.random.randint(jax.random.fold_in(key, 1), (pairs,), 0, 1 << 20) % (room + 1)
    tallies = tallies.at[1:1 + 2 * pairs:2].set(giver - passed).at[2:2 + 2 * pairs:2].set(sink + passed)
    return tallies[jax.random.permutation(jax.random.fold_in(key, 2), amount)]


def normal_values(own_key, shape, deviation, limit, cuts=(), kind=jnp.bfloat16):
    values = deviation * jax.random.normal(own_key, shape, jnp.float32)
    if cuts:
        values = values * levels(own_key, shape, cuts, -0.22, 0.18)
    return jnp.clip(values, -limit, limit).astype(kind)


def setup_inputs(seed: int = 0, part: int = 0) -> dict:
    streams_of = jax.random.split(jax.random.key(seed), 9)
    own_keys = jax.random.split(jax.random.fold_in(streams_of[8], part), 9)
    return {
        "tokens": draw_tokens(jax.random.fold_in(jax.random.fold_in(streams_of[8], part), 71), part),
        "query_base_weight": normal_values(streams_of[1], (MODEL_WIDTH, QUERY_WIDTH), MODEL_WIDTH ** -0.5, 0.0625, ((0, 4), (1, 4))),
        "adapter_down_weight": normal_values(streams_of[2], (ADAPTER_COUNT, MODEL_WIDTH, ADAPTER_RANK), MODEL_WIDTH ** -0.5, 0.0625, ((0, 4), (1, 4))),
        "adapter_up_weight": normal_values(streams_of[3], (ADAPTER_COUNT, ADAPTER_RANK, QUERY_WIDTH), ADAPTER_RANK ** -0.5, 0.75, ((0, 4), (2, 4))),
        "rotated_key_cache": draw_rotated_key_cache(jax.random.fold_in(jax.random.fold_in(streams_of[8], part), 71), part),
        "value_cache_rows": normal_values(own_keys[5], (TOKENS, KVH, HD), 1.0, 6.0, ((0, 4),)),
        "segment_index": jax.vmap(lambda own: jnp.searchsorted(jnp.cumsum(uneven_parts(own, SEQUENCE_COUNT, TOK_DEV, MOST, 2)), jnp.arange(TOK_DEV), side="right"))(jax.random.split(own_keys[6], BATCHES)).reshape((BATCHES, TOK_DEV)).astype(jnp.int32),
        "tenant_index": draw_tenant_index(jax.random.fold_in(jax.random.fold_in(streams_of[8], part), 71), part),
    }


rope_theta = 500000.0
adapter_scale = 0.5

def positions_of(segment_row):
    length = segment_row.shape[0]
    indices = jnp.arange(length, dtype=jnp.int32)
    starting = jnp.concatenate([jnp.ones((1,), jnp.bool_), segment_row[1:] != segment_row[:-1]])
    earliest = lax.cummax(jnp.where(starting, indices, jnp.zeros_like(indices)), axis=0)
    return (indices - earliest).astype(jnp.float32)

def rotate(matrix, position):
    half_width = matrix.shape[-1] // 2
    exponent = jnp.arange(half_width, dtype=jnp.float32) * (2.0 / matrix.shape[-1])
    frequency = jnp.power(jnp.float32(rope_theta), -exponent)
    angles = position[:, None] * frequency[None, :]
    cosine = jnp.cos(angles)
    sine = jnp.sin(angles)
    leading = matrix[..., :half_width]
    trailing = matrix[..., half_width:]
    return jnp.concatenate([leading * cosine - trailing * sine, trailing * cosine + leading * sine], axis=-1)

def attend(query_head, key_head, value_head, segment_row):
    length = segment_row.shape[0]
    indices = jnp.arange(length, dtype=jnp.int32)
    scores = jnp.dot(query_head, key_head.T, preferred_element_type=jnp.float32) * (1.0 / jnp.sqrt(jnp.float32(query_head.shape[-1])))
    allowed = (segment_row[:, None] == segment_row[None, :]) & (indices[None, :] <= indices[:, None])
    masked = jnp.where(allowed, scores, -jnp.inf)
    highest = lax.optimization_barrier(jnp.max(masked, axis=1, keepdims=True))
    expanded = jnp.where(allowed, jnp.exp(scores - highest), jnp.float32(0.0))
    totals = lax.optimization_barrier(jnp.sum(expanded, axis=1, keepdims=True))
    probs = (expanded / totals).astype(jnp.bfloat16)
    return jnp.dot(probs, value_head, preferred_element_type=jnp.float32).astype(jnp.bfloat16)

def reference(tokens, query_base_weight, adapter_down_weight, adapter_up_weight, rotated_key_cache, value_cache_rows, segment_index, tenant_index):
    group_size = HEADS // KVH
    results = []
    for batch in range(BATCHES):
        lower = batch * TOK_DEV
        token_rows = tokens[lower:lower + TOK_DEV]
        segment_row = segment_index[batch]
        token_tenants = tenant_index[batch]
        onehot = (segment_row[:, None] == jnp.arange(SEQUENCE_COUNT, dtype=jnp.int32)[None, :]).astype(jnp.float32)
        base_output = jnp.dot(token_rows, query_base_weight, preferred_element_type=jnp.float32)
        selected_down = adapter_down_weight[token_tenants]
        down_flat = jnp.transpose(selected_down, (1, 0, 2)).reshape(MODEL_WIDTH, SEQUENCE_COUNT * ADAPTER_RANK)
        shrink_all = jnp.dot(token_rows, down_flat, preferred_element_type=jnp.float32).reshape(TOK_DEV, SEQUENCE_COUNT, ADAPTER_RANK)
        shrink = lax.optimization_barrier(jnp.sum(onehot[:, :, None] * shrink_all, axis=1))
        shrink_b = shrink.astype(jnp.bfloat16)
        spread = (onehot[:, :, None] * shrink_b.astype(jnp.float32)[:, None, :]).astype(jnp.bfloat16)
        flattened_up = adapter_up_weight[token_tenants].reshape(SEQUENCE_COUNT * ADAPTER_RANK, QUERY_WIDTH)
        adapted_queries = jnp.dot(spread.reshape(TOK_DEV, SEQUENCE_COUNT * ADAPTER_RANK), flattened_up, preferred_element_type=jnp.float32)
        combined_queries = base_output + adapter_scale * adapted_queries
        per_head = jnp.transpose(combined_queries.reshape(TOK_DEV, HEADS, HD), (1, 0, 2))
        queries = rotate(per_head, positions_of(segment_row)).astype(jnp.bfloat16)
        key_rows = jnp.transpose(jnp.repeat(rotated_key_cache[lower:lower + TOK_DEV], group_size, axis=1), (1, 0, 2))
        value_rows = jnp.transpose(jnp.repeat(value_cache_rows[lower:lower + TOK_DEV], group_size, axis=1), (1, 0, 2))

        def one_head(operands):
            return attend(operands[0], operands[1], operands[2], segment_row)
        heads_out = lax.map(one_head, (queries, key_rows, value_rows))
        results.append(jnp.transpose(heads_out, (1, 0, 2)).reshape(TOK_DEV, QUERY_WIDTH))
    return jnp.concatenate(results, axis=0)
```

```python
import math

import jax
import jax.numpy as jnp
import numpy as np
from jax import lax
from jax.experimental import pallas as pl
from jax.experimental.pallas import tpu as pltpu
from jax.sharding import PartitionSpec as P

rope_theta = 500000.0
adapter_scale = 0.5
SLOTS = 4
MESH = pl.DeviceIdType.MESH


def positions_of(segment_row):
    length = segment_row.shape[0]
    indices = jnp.arange(length, dtype=jnp.int32)
    starting = jnp.concatenate([jnp.ones((1,), jnp.bool_), segment_row[1:] != segment_row[:-1]])
    earliest = lax.cummax(jnp.where(starting, indices, jnp.zeros_like(indices)), axis=0)
    return (indices - earliest).astype(jnp.float32)


def rotate(matrix, position):
    half_width = matrix.shape[-1] // 2
    exponent = jnp.arange(half_width, dtype=jnp.float32) * (2.0 / matrix.shape[-1])
    frequency = jnp.power(jnp.float32(rope_theta), -exponent)
    angles = position[:, None] * frequency[None, :]
    cosine = jnp.cos(angles)
    sine = jnp.sin(angles)
    leading = matrix[..., :half_width]
    trailing = matrix[..., half_width:]
    return jnp.concatenate(
        [leading * cosine - trailing * sine, trailing * cosine + leading * sine], axis=-1
    )


def attend(query_head, key_head, value_head, segment_row):
    length = segment_row.shape[0]
    indices = jnp.arange(length, dtype=jnp.int32)
    scores = jnp.dot(query_head, key_head.T, preferred_element_type=jnp.float32) * (
        1.0 / jnp.sqrt(jnp.float32(query_head.shape[-1]))
    )
    allowed = (segment_row[:, None] == segment_row[None, :]) & (
        indices[None, :] <= indices[:, None]
    )
    masked = jnp.where(allowed, scores, -jnp.inf)
    highest = jnp.max(masked, axis=1, keepdims=True)
    expanded = jnp.where(allowed, jnp.exp(scores - highest), jnp.float32(0.0))
    totals = jnp.sum(expanded, axis=1, keepdims=True)
    probs = (expanded / totals).astype(jnp.bfloat16)
    return jnp.dot(probs, value_head, preferred_element_type=jnp.float32).astype(jnp.bfloat16)


def body(
    tokens,
    query_base_weight,
    adapter_down_weight,
    adapter_up_weight,
    rotated_key_cache,
    value_cache_rows,
    segment_index,
    tenant_index,
):
    segment_row = segment_index[0]
    token_tenants = tenant_index[0]
    sequences = token_tenants.shape[0]
    row_count = tokens.shape[0]
    adapter_rank_width = adapter_down_weight.shape[2]
    head_width = query_base_weight.shape[1]
    feature_matrix = adapter_down_weight.shape[1]
    onehot = segment_row[:, None] == jnp.arange(sequences, dtype=jnp.int32)[None, :]
    gathered = lax.all_gather(tokens, "tp", axis=1, tiled=True)
    base_output = jnp.dot(
        gathered,
        lax.all_gather(query_base_weight, "ad", axis=0, tiled=True),
        preferred_element_type=jnp.float32,
    )
    portions = (
        lax.all_gather(adapter_down_weight, "ad", axis=0, tiled=True),
        lax.all_gather(adapter_up_weight, "ad", axis=0, tiled=True),
    )
    count = portions[0].shape[0]
    lookup = (token_tenants[:, None] == jnp.arange(count, dtype=jnp.int32)[None, :]).astype(
        jnp.bfloat16
    )
    down_part = jnp.einsum("sn,nxr->sxr", lookup, portions[0], preferred_element_type=jnp.float32)
    up_part = jnp.einsum("sn,nrh->srh", lookup, portions[1], preferred_element_type=jnp.float32)
    selected_down = down_part.astype(jnp.bfloat16)
    up_sel = up_part.astype(jnp.bfloat16)
    selected_down, up_sel = (selected_down, up_sel)
    down_flat = jnp.transpose(selected_down, (1, 0, 2)).reshape(
        feature_matrix, sequences * adapter_rank_width
    )
    partial_all = jnp.dot(tokens, down_flat, preferred_element_type=jnp.float32).reshape(
        row_count, sequences, adapter_rank_width
    )
    partial_sum = jnp.sum(jnp.where(onehot[:, :, None], partial_all, jnp.float32(0.0)), axis=1)
    shrink_b = lax.psum(partial_sum, "tp").astype(jnp.bfloat16)
    spread = jnp.where(onehot[:, :, None], shrink_b[:, None, :], jnp.zeros((), jnp.bfloat16))
    flat_rows = spread.reshape(row_count, sequences * adapter_rank_width)
    adapted_queries = jnp.dot(
        flat_rows,
        up_sel.reshape(sequences * adapter_rank_width, head_width),
        preferred_element_type=jnp.float32,
    )
    combined_queries = base_output + adapter_scale * adapted_queries
    queries = rotate(combined_queries, positions_of(segment_row)).astype(jnp.bfloat16)
    heads_total = lax.axis_size("tp")
    kv_heads = rotated_key_cache.shape[1]
    kv_index = lax.axis_index("tp") // (heads_total // kv_heads)
    key_head = lax.dynamic_index_in_dim(rotated_key_cache, kv_index, 1, keepdims=False)
    value_head = lax.dynamic_index_in_dim(value_cache_rows, kv_index, 1, keepdims=False)
    return attend(queries, key_head, value_head, segment_row)


def fused_kernel(
    tok_hbm,
    w_hbm,
    down_hbm,
    up_ref,
    key_ref,
    value_ref,
    seg_ref,
    tenant_ref,
    freq_ref,
    out_ref,
    tok,
    down,
    weight,
    send_a,
    recv_a,
    send_u,
    recv_u,
    tenants,
    tenant_smem,
    part_send,
    part_recv,
    slot_col,
    cosine,
    sine,
    shrink,
    packed,
    quarter_recv,
    rounded,
    local_sem,
    ten_send,
    ten_recv,
    ws1,
    ws2,
    w_recv,
    a_send,
    a_recv,
    u_send,
    u_recv,
    p_send,
    p_recv,
    q_send,
    q_recv,
    g_send,
    g_recv,
):
    rep, tp, ad = lax.axis_index("rep"), lax.axis_index("tp"), lax.axis_index("ad")
    rows, depth = tok.shape
    rank = down.shape[1]
    held_count = down.shape[0]
    head = weight.shape[2]
    sequences = SLOTS * 2
    core = lax.rem(ad, 2)
    mate = ad + 1 - 2 * core
    far0 = lax.rem(ad + 2, 4)
    far1 = far0 + 1 - 2 * lax.rem(far0, 2)
    other_rep = 1 - rep
    lane = lax.broadcasted_iota(jnp.int32, (rows, 128), 1)
    lane_half = lane // rank

    def remote(src, dst, ss, rs, r=None, t=None, a=None):
        return pltpu.make_async_remote_copy(
            src_ref=src,
            dst_ref=dst,
            send_sem=ss,
            recv_sem=rs,
            device_id=(rep if r is None else r, tp if t is None else t, ad if a is None else a),
            device_id_type=MESH,
        )

    load_down = pltpu.make_async_copy(down_hbm, down, local_sem.at[0])
    load_tok = pltpu.make_async_copy(tok_hbm, tok, local_sem.at[1])
    load_down.start()
    load_tok.start()

    barrier = pltpu.get_barrier_semaphore()
    for dt in range(4):
        for da in range(4):
            if dt or da:
                pl.semaphore_signal(
                    barrier,
                    inc=1,
                    device_id=(rep, lax.rem(tp + dt, 4), lax.rem(ad + da, 4)),
                    device_id_type=MESH,
                )
    pl.semaphore_signal(barrier, inc=1, device_id=(other_rep, tp, ad), device_id_type=MESH)
    pl.semaphore_wait(barrier, 16)

    tenants[ad] = tenant_ref[...]
    for d in range(1, 4):
        peer = lax.rem(ad + d, 4)
        remote(tenant_ref, tenants.at[ad], ten_send.at[peer], ten_recv.at[ad], a=peer).start()

    part = depth // 4

    def quarter(q):
        return pl.ds(pl.multiple_of(q * part, part), part)

    for target in range(4):
        rows_q = quarter(rep * 2 + target % 2)
        q = rep * 2 + target % 2
        mine = jnp.logical_and(tp == ad, ad == target)

        @pl.when(mine)
        def _():
            pltpu.make_async_copy(
                w_hbm.at[rows_q], weight.at[tp, rows_q], w_recv.at[tp, q]
            ).start()

        @pl.when(jnp.logical_not(mine))
        def _():
            remote(
                w_hbm.at[rows_q],
                weight.at[tp, rows_q],
                ws1.at[target],
                w_recv.at[tp, q],
                t=ad,
                a=target,
            ).start()

    seg_row = seg_ref[...]
    seg_col = jnp.transpose(
        jnp.broadcast_to(seg_row.astype(jnp.float32), (128, rows)), (1, 0)
    ).astype(jnp.int32)

    for d in range(1, 4):
        peer = lax.rem(ad + d, 4)
        remote(tenant_ref, tenants.at[peer], ten_send.at[peer], ten_recv.at[peer], a=peer).wait()
    to_smem = pltpu.make_async_copy(tenants, tenant_smem, local_sem.at[2])
    to_smem.start()
    to_smem.wait()
    load_down.wait()

    def picks(batch):
        chosen = [jnp.int32(0)] * SLOTS
        count = jnp.int32(0)
        for s in range(sequences):
            number = tenant_smem[batch, 0, s]
            here = number // held_count == ad
            for c in range(SLOTS):
                chosen[c] = jnp.where(
                    jnp.logical_and(here, count == c), lax.rem(number, held_count), chosen[c]
                )
            count = count + here.astype(jnp.int32)
        return chosen

    def fill(target_a, target_u, chosen, pair):
        for c in (2 * pair, 2 * pair + 1):
            target_a[pl.ds(c * rank, rank), :] = down[chosen[c]]
            target_u[pl.ds(c * rank, rank), :] = up_ref[chosen[c]]

    def half(ref, owner, pair):
        return ref.at[owner, pl.ds(pair * 2 * rank, 2 * rank)]

    picked = {}
    for pair in range(2):
        for name, peer in (("far0", far0), ("far1", far1)):
            if pair == 0:
                picked[name] = picks(peer)
            fill(send_a.at[peer], send_u.at[peer], picked[name], pair)
            remote(
                half(send_a, peer, pair),
                half(recv_a, ad, pair),
                a_send.at[peer, pair],
                a_recv.at[ad, pair],
                a=peer,
            ).start()
    picked["mate"] = picks(mate)
    for pair in range(2):
        fill(send_a.at[mate], send_u.at[mate], picked["mate"], pair)
        remote(
            half(send_a, mate, pair),
            half(recv_a, ad, pair),
            a_send.at[mate, pair],
            a_recv.at[ad, pair],
            a=mate,
        ).start()
    for peer in (far0, far1, mate):
        remote(
            send_u.at[peer], recv_u.at[ad], u_send.at[peer], u_recv.at[ad], a=peer
        ).start()

    q_own, q_mate = rep * 2 + core, rep * 2 + 1 - core
    y_own, y_mate = other_rep * 2 + core, other_rep * 2 + 1 - core

    def w_wait(t, q):
        remote(
            weight.at[t, quarter(q)], weight.at[t, quarter(q)], ws1.at[0], w_recv.at[t, q], a=mate
        ).wait_recv()

    def forward(t, q, k, to_rep):
        block = weight.at[t, quarter(q)]
        if to_rep:
            return remote(block, block, ws2.at[t, k], w_recv.at[t, q], r=other_rep)
        return remote(block, block, ws2.at[t, k], w_recv.at[t, q], a=mate)

    for d in range(4):
        t = lax.rem(tp + d, 4)
        w_wait(t, q_own)
        forward(t, q_own, 0, True).start()
        forward(t, q_own, 1, False).start()

    picked["own"] = picks(ad)
    for pair in range(2):
        fill(recv_a.at[ad], recv_u.at[ad], picked["own"], pair)

    starts = jnp.zeros((rows, 128), jnp.int32)
    slots = jnp.zeros((rows, 128), jnp.int32)
    for s in range(sequences):
        number = tenant_smem[ad, 0, s]
        owner = number // held_count
        before = jnp.int32(0)
        for e in range(s):
            before = before + (tenant_smem[ad, 0, e] // held_count == owner).astype(jnp.int32)
        first = jnp.sum((seg_row < s).astype(jnp.float32), axis=1, keepdims=True)
        hit = seg_col == s
        slots = jnp.where(hit, owner * SLOTS + before, slots)
        starts = jnp.where(hit, first.astype(jnp.int32), starts)
    slot_col[...] = slots
    position = (lax.broadcasted_iota(jnp.int32, (rows, 128), 0) - starts).astype(jnp.float32)
    angles = position * freq_ref[...]
    cosine[...] = jnp.cos(angles)
    sine[...] = jnp.where(lane_half == 0, -jnp.sin(angles), jnp.sin(angles))
    load_tok.wait()
    shrink[...] = jnp.zeros_like(shrink)

    for d in range(4):
        t = lax.rem(tp + d, 4)
        w_wait(t, y_own)
        forward(t, y_own, 2, False).start()

    tile = 256
    NT = (((1,), (1,)), ((), ()))

    def base_product(t, target):
        @pl.loop(0, rows // tile)
        def _(m):
            at = pl.ds(pl.multiple_of(m * tile, tile), tile)
            target[at, :] = jnp.dot(tok[at, :], weight[t], preferred_element_type=jnp.float32)

    for d in (1, 2, 3, 0):
        t = lax.rem(tp + d, 4)
        w_wait(t, q_mate)
        w_wait(t, y_mate)
        if d:
            base_product(t, part_send.at[t])
            remote(part_send.at[t], part_recv.at[tp], p_send.at[t], p_recv.at[tp], t=t).start()
        else:
            base_product(t, part_recv.at[tp])

    def shrink_product(owner, pair):
        @pl.loop(0, rows // tile)
        def _(m):
            at = pl.ds(pl.multiple_of(m * tile, tile), tile)
            product = lax.dot_general(
                tok[at, :],
                recv_a[owner, pl.ds(pair * 2 * rank, 2 * rank), :],
                NT,
                preferred_element_type=jnp.float32,
            )
            wanted = owner * SLOTS + pair * 2 + lane_half[:tile]
            shrink[at, :] = jnp.where(slot_col[at, :] == wanted, product, shrink[at, :])

    def a_wait(owner, pair):
        remote(
            half(recv_a, owner, pair),
            half(recv_a, owner, pair),
            a_send.at[owner, pair],
            a_recv.at[owner, pair],
            a=owner,
        ).wait_recv()

    for pair in range(2):
        shrink_product(ad, pair)
    for pair in range(2):
        a_wait(mate, pair)
        shrink_product(mate, pair)
    for pair in range(2):
        for owner in (far0, far1):
            a_wait(owner, pair)
            shrink_product(owner, pair)

    both = shrink[...] + pltpu.roll(shrink[...], rank, 1)
    low = rows // 2
    packed[...] = jnp.where(lane_half[:low] == 0, both[:low], both[low:])
    span = low // 4

    def piece(t):
        return pl.ds(pl.multiple_of(t * span, span), span)

    for d in range(1, 4):
        t = lax.rem(tp + d, 4)
        remote(packed.at[piece(t)], quarter_recv.at[tp], q_send.at[t], q_recv.at[tp], t=t).start()
    quarter_recv[tp] = packed[piece(tp), :]
    for d in range(1, 4):
        t = lax.rem(tp + d, 4)
        remote(packed.at[piece(t)], quarter_recv.at[t], q_send.at[t], q_recv.at[t], t=t).wait_recv()
    total = (quarter_recv[0] + quarter_recv[1]) + (quarter_recv[2] + quarter_recv[3])
    rounded[tp] = total.astype(jnp.bfloat16)
    for d in range(1, 4):
        t = lax.rem(tp + d, 4)
        remote(rounded.at[tp], rounded.at[tp], g_send.at[t], g_recv.at[tp], t=t).start()

    for d in range(1, 4):
        t = lax.rem(tp + d, 4)
        remote(part_send.at[t], part_recv.at[t], p_send.at[t], p_recv.at[t], t=t).wait()
        peer = lax.rem(ad + d, 4)
        remote(send_u.at[peer], recv_u.at[peer], u_send.at[peer], u_recv.at[peer], a=peer).wait()
        remote(packed.at[piece(t)], quarter_recv.at[t], q_send.at[t], q_recv.at[t], t=t).wait_send()
        for pair in range(2):
            remote(
                half(send_a, peer, pair),
                half(recv_a, peer, pair),
                a_send.at[peer, pair],
                a_recv.at[peer, pair],
                a=peer,
            ).wait_send()
    for d in range(4):
        forward(d, q_own, 0, True).wait_send()
        forward(d, q_own, 1, False).wait_send()
        forward(d, y_own, 2, False).wait_send()
    for target in range(4):
        rows_q = quarter(rep * 2 + target % 2)
        mine = jnp.logical_and(tp == ad, ad == target)

        @pl.when(jnp.logical_not(mine))
        def _():
            remote(
                w_hbm.at[rows_q],
                weight.at[tp, rows_q],
                ws1.at[target],
                w_recv.at[tp, rep * 2 + target % 2],
                t=ad,
                a=target,
            ).wait_send()

    for d in range(1, 4):
        t = lax.rem(tp + d, 4)
        remote(rounded.at[t], rounded.at[t], g_send.at[t], g_recv.at[t], t=t).wait()

    scale = 1.0 / math.sqrt(head)
    half_low = lane_half[:span]
    top, bottom = [], []
    for t in range(4):
        values = rounded[t].astype(jnp.float32)
        turned = pltpu.roll(values, rank, 1)
        top.append(jnp.where(half_low == 0, values, turned))
        bottom.append(jnp.where(half_low == 0, turned, values))
    shrink[...] = jnp.concatenate(top + bottom, axis=0)

    for start in range(0, rows, tile):
        at = pl.ds(start, tile)
        slots_here = slot_col[at, :]
        shrink_here = shrink[at, :]
        adapted = jnp.zeros((tile, head), jnp.float32)
        for owner in range(4):
            for pair in range(2):
                wanted = owner * SLOTS + pair * 2 + lane_half[:tile]
                spread = jnp.where(slots_here == wanted, shrink_here, 0.0).astype(jnp.bfloat16)
                adapted = adapted + jnp.dot(
                    spread,
                    recv_u[owner, pl.ds(pair * 2 * rank, 2 * rank), :],
                    preferred_element_type=jnp.float32,
                )
        base = (part_recv[0, at, :] + part_recv[1, at, :]) + (
            part_recv[2, at, :] + part_recv[3, at, :]
        )
        combined = base + adapter_scale * adapted
        queries = (
            combined * cosine[at, :] + pltpu.roll(combined, head // 2, 1) * sine[at, :]
        ).astype(jnp.bfloat16)
        first = max(0, start - tile)
        width = start + tile - first
        scores = (
            lax.dot_general(
                queries, key_ref[pl.ds(first, width), :], NT, preferred_element_type=jnp.float32
            )
            * scale
        )
        row_at = start + lax.broadcasted_iota(jnp.int32, (tile, width), 0)
        col_at = first + lax.broadcasted_iota(jnp.int32, (tile, width), 1)
        row_seg = jnp.transpose(
            jnp.broadcast_to(seg_row[:, start : start + tile].astype(jnp.float32), (128, tile)),
            (1, 0),
        )[:, :1].astype(jnp.int32)
        allowed = jnp.logical_and(row_seg == seg_row[:, first : first + width], col_at <= row_at)
        masked = jnp.where(allowed, scores, -jnp.inf)
        highest = jnp.max(masked, axis=1, keepdims=True)
        expanded = jnp.where(allowed, jnp.exp(scores - highest), 0.0)
        probs = (expanded / jnp.sum(expanded, axis=1, keepdims=True)).astype(jnp.bfloat16)
        out_ref[at, :] = jnp.dot(
            probs, value_ref[pl.ds(first, width), :], preferred_element_type=jnp.float32
        ).astype(jnp.bfloat16)


def fused_body(
    tokens,
    query_base_weight,
    adapter_down_weight,
    adapter_up_weight,
    rotated_key_cache,
    value_cache_rows,
    segment_index,
    tenant_index,
):
    rows, depth = tokens.shape
    held, _, rank = adapter_down_weight.shape
    head = query_base_weight.shape[1]
    kv_index = lax.axis_index("tp") // (lax.axis_size("tp") // rotated_key_cache.shape[1])
    key_head = lax.dynamic_index_in_dim(rotated_key_cache, kv_index, 1, keepdims=False)
    value_head = lax.dynamic_index_in_dim(value_cache_rows, kv_index, 1, keepdims=False)
    tenant_tile = jnp.pad(tenant_index, ((0, 7), (0, 128 - tenant_index.shape[1])))
    exponent = np.arange(head // 2, dtype=np.float32) * np.float32(2.0 / head)
    frequency = np.power(np.float32(rope_theta), -exponent).astype(np.float32)
    freq_row = jnp.asarray(np.concatenate([frequency, frequency])[None, :])
    bf16, f32 = jnp.bfloat16, jnp.float32
    DMA = pltpu.SemaphoreType.DMA
    vmem = pl.BlockSpec(memory_space=pltpu.VMEM)
    anywhere = pl.BlockSpec(memory_space=pl.ANY)
    return pl.pallas_call(
        fused_kernel,
        out_shape=jax.ShapeDtypeStruct((rows, head), bf16),
        in_specs=[anywhere] * 3 + [vmem] * 6,
        out_specs=vmem,
        scratch_shapes=[
            pltpu.VMEM((rows, depth), bf16),
            pltpu.VMEM((held, rank, depth), bf16),
            pltpu.VMEM((4, depth, head), bf16),
            pltpu.VMEM((4, SLOTS * rank, depth), bf16),
            pltpu.VMEM((4, SLOTS * rank, depth), bf16),
            pltpu.VMEM((4, SLOTS * rank, head), bf16),
            pltpu.VMEM((4, SLOTS * rank, head), bf16),
            pltpu.VMEM((4, 8, 128), jnp.int32),
            pltpu.SMEM((4, 8, 128), jnp.int32),
            pltpu.VMEM((4, rows, head), f32),
            pltpu.VMEM((4, rows, head), f32),
            pltpu.VMEM((rows, 128), jnp.int32),
            pltpu.VMEM((rows, 128), f32),
            pltpu.VMEM((rows, 128), f32),
            pltpu.VMEM((rows, 128), f32),
            pltpu.VMEM((rows // 2, 128), f32),
            pltpu.VMEM((4, rows // 8, 128), f32),
            pltpu.VMEM((4, rows // 8, 128), bf16),
            DMA((3,)),
            DMA((4,)),
            DMA((4,)),
            DMA((4,)),
            DMA((4, 3)),
            DMA((4, 4)),
            DMA((4, 2)),
            DMA((4, 2)),
            DMA((4,)),
            DMA((4,)),
            DMA((4,)),
            DMA((4,)),
            DMA((4,)),
            DMA((4,)),
            DMA((4,)),
            DMA((4,)),
        ],
        compiler_params=pltpu.CompilerParams(
            collective_id=0, has_side_effects=True, vmem_limit_bytes=56 * 1024 * 1024
        ),
        cost_estimate=pl.CostEstimate(
            flops=2 * rows * depth * 12 * head, bytes_accessed=20 << 20, transcendentals=1 << 20
        ),
    )(
        tokens,
        query_base_weight,
        jnp.transpose(adapter_down_weight, (0, 2, 1)),
        adapter_up_weight,
        key_head,
        value_head,
        segment_index,
        tenant_tile,
        freq_row,
    )


def solution(mesh):
    square = dict(mesh.shape) == {"rep": 2, "tp": 4, "ad": 4}
    return jax.shard_map(
        fused_body if square else body,
        mesh=mesh,
        in_specs=(
            P(("rep", "ad"), "tp"),
            P("ad", "tp"),
            P("ad", "tp", None),
            P("ad", None, "tp"),
            P(("rep", "ad"), None, None),
            P(("rep", "ad"), None, None),
            P(("rep", "ad"), None),
            P(("rep", "ad"), None),
        ),
        out_specs=P(("rep", "ad"), "tp"),
        check_vma=False,
    )
```

```python
import math

import jax
import jax.numpy as jnp
import numpy as np
from jax import lax
from jax.experimental import pallas as pl
from jax.experimental.pallas import tpu as pltpu
from jax.sharding import PartitionSpec as P

rope_theta = 500000.0
adapter_scale = 0.5
SLOTS = 4
MESH = pl.DeviceIdType.MESH


def positions_of(segment_row):
    length = segment_row.shape[0]
    indices = jnp.arange(length, dtype=jnp.int32)
    starting = jnp.concatenate([jnp.ones((1,), jnp.bool_), segment_row[1:] != segment_row[:-1]])
    earliest = lax.cummax(jnp.where(starting, indices, jnp.zeros_like(indices)), axis=0)
    return (indices - earliest).astype(jnp.float32)


def rotate(matrix, position):
    half_width = matrix.shape[-1] // 2
    exponent = jnp.arange(half_width, dtype=jnp.float32) * (2.0 / matrix.shape[-1])
    frequency = jnp.power(jnp.float32(rope_theta), -exponent)
    angles = position[:, None] * frequency[None, :]
    cosine = jnp.cos(angles)
    sine = jnp.sin(angles)
    leading = matrix[..., :half_width]
    trailing = matrix[..., half_width:]
    return jnp.concatenate(
        [leading * cosine - trailing * sine, trailing * cosine + leading * sine], axis=-1
    )


def attend(query_head, key_head, value_head, segment_row):
    length = segment_row.shape[0]
    indices = jnp.arange(length, dtype=jnp.int32)
    scores = jnp.dot(query_head, key_head.T, preferred_element_type=jnp.float32) * (
        1.0 / jnp.sqrt(jnp.float32(query_head.shape[-1]))
    )
    allowed = (segment_row[:, None] == segment_row[None, :]) & (
        indices[None, :] <= indices[:, None]
    )
    masked = jnp.where(allowed, scores, -jnp.inf)
    highest = jnp.max(masked, axis=1, keepdims=True)
    expanded = jnp.where(allowed, jnp.exp(scores - highest), jnp.float32(0.0))
    totals = jnp.sum(expanded, axis=1, keepdims=True)
    probs = (expanded / totals).astype(jnp.bfloat16)
    return jnp.dot(probs, value_head, preferred_element_type=jnp.float32).astype(jnp.bfloat16)


def body(
    tokens,
    query_base_weight,
    adapter_down_weight,
    adapter_up_weight,
    rotated_key_cache,
    value_cache_rows,
    segment_index,
    tenant_index,
):
    segment_row = segment_index[0]
    token_tenants = tenant_index[0]
    sequences = token_tenants.shape[0]
    row_count = tokens.shape[0]
    adapter_rank_width = adapter_down_weight.shape[2]
    head_width = query_base_weight.shape[1]
    feature_matrix = adapter_down_weight.shape[1]
    onehot = segment_row[:, None] == jnp.arange(sequences, dtype=jnp.int32)[None, :]
    gathered = lax.all_gather(tokens, "tp", axis=1, tiled=True)
    base_output = jnp.dot(
        gathered,
        lax.all_gather(query_base_weight, "ad", axis=0, tiled=True),
        preferred_element_type=jnp.float32,
    )
    portions = (
        lax.all_gather(adapter_down_weight, "ad", axis=0, tiled=True),
        lax.all_gather(adapter_up_weight, "ad", axis=0, tiled=True),
    )
    count = portions[0].shape[0]
    lookup = (token_tenants[:, None] == jnp.arange(count, dtype=jnp.int32)[None, :]).astype(
        jnp.bfloat16
    )
    down_part = jnp.einsum("sn,nxr->sxr", lookup, portions[0], preferred_element_type=jnp.float32)
    up_part = jnp.einsum("sn,nrh->srh", lookup, portions[1], preferred_element_type=jnp.float32)
    selected_down = down_part.astype(jnp.bfloat16)
    up_sel = up_part.astype(jnp.bfloat16)
    selected_down, up_sel = (selected_down, up_sel)
    down_flat = jnp.transpose(selected_down, (1, 0, 2)).reshape(
        feature_matrix, sequences * adapter_rank_width
    )
    partial_all = jnp.dot(tokens, down_flat, preferred_element_type=jnp.float32).reshape(
        row_count, sequences, adapter_rank_width
    )
    partial_sum = jnp.sum(jnp.where(onehot[:, :, None], partial_all, jnp.float32(0.0)), axis=1)
    shrink_b = lax.psum(partial_sum, "tp").astype(jnp.bfloat16)
    spread = jnp.where(onehot[:, :, None], shrink_b[:, None, :], jnp.zeros((), jnp.bfloat16))
    flat_rows = spread.reshape(row_count, sequences * adapter_rank_width)
    adapted_queries = jnp.dot(
        flat_rows,
        up_sel.reshape(sequences * adapter_rank_width, head_width),
        preferred_element_type=jnp.float32,
    )
    combined_queries = base_output + adapter_scale * adapted_queries
    queries = rotate(combined_queries, positions_of(segment_row)).astype(jnp.bfloat16)
    heads_total = lax.axis_size("tp")
    kv_heads = rotated_key_cache.shape[1]
    kv_index = lax.axis_index("tp") // (heads_total // kv_heads)
    key_head = lax.dynamic_index_in_dim(rotated_key_cache, kv_index, 1, keepdims=False)
    value_head = lax.dynamic_index_in_dim(value_cache_rows, kv_index, 1, keepdims=False)
    return attend(queries, key_head, value_head, segment_row)


def fused_kernel(
    tok_hbm,
    w_hbm,
    down_hbm,
    up_ref,
    key_ref,
    value_ref,
    seg_ref,
    tenant_ref,
    freq_ref,
    cos_ref,
    sin_ref,
    out_ref,
    tok,
    down,
    weight,
    send_a,
    recv_a,
    send_u,
    recv_u,
    tenants,
    tenant_smem,
    part_send,
    part_recv,
    part_own,
    wide_send,
    wide_recv,
    slot_col,
    cosine,
    sine,
    shrink,
    packed,
    quarter_recv,
    rounded,
    key_head,
    value_head,
    local_sem,
    ten_send,
    ten_recv,
    ws1,
    ws2,
    w_recv,
    a_send,
    a_recv,
    u_send,
    u_recv,
    p_send,
    p_recv,
    q_send,
    q_recv,
    g_send,
    g_recv,
):
    rep, tp, ad = lax.axis_index("rep"), lax.axis_index("tp"), lax.axis_index("ad")
    rows, depth = tok.shape
    rank = down.shape[1]
    held_count = down.shape[0]
    head = weight.shape[2]
    sequences = SLOTS * 2
    core = lax.rem(ad, 2)
    mate = ad + 1 - 2 * core
    far0 = lax.rem(ad + 2, 4)
    far1 = far0 + 1 - 2 * lax.rem(far0, 2)
    other_rep = 1 - rep
    lane = lax.broadcasted_iota(jnp.int32, (rows, 128), 1)
    lane_half = lane // rank

    def remote(src, dst, ss, rs, r=None, t=None, a=None):
        return pltpu.make_async_remote_copy(
            src_ref=src,
            dst_ref=dst,
            send_sem=ss,
            recv_sem=rs,
            device_id=(rep if r is None else r, tp if t is None else t, ad if a is None else a),
            device_id_type=MESH,
        )

    load_down = pltpu.make_async_copy(down_hbm, down, local_sem.at[0])
    load_tok = pltpu.make_async_copy(tok_hbm, tok, local_sem.at[1])
    load_down.start()
    load_tok.start()

    barrier = pltpu.get_barrier_semaphore()
    for dt in range(4):
        for da in range(4):
            if dt or da:
                pl.semaphore_signal(
                    barrier,
                    inc=1,
                    device_id=(rep, lax.rem(tp + dt, 4), lax.rem(ad + da, 4)),
                    device_id_type=MESH,
                )
    pl.semaphore_signal(barrier, inc=1, device_id=(other_rep, tp, ad), device_id_type=MESH)
    pl.semaphore_wait(barrier, 16)

    tenants[ad] = jnp.zeros(tenants.shape[1:], jnp.int32)
    tenants[ad, 0:1, 0 : tenant_ref.shape[1]] = tenant_ref[...]
    for d in range(1, 4):
        peer = lax.rem(ad + d, 4)
        remote(tenants.at[ad], tenants.at[ad], ten_send.at[peer], ten_recv.at[ad], a=peer).start()

    part = depth // 4

    def quarter(q):
        return pl.ds(pl.multiple_of(q * part, part), part)

    for target in range(4):
        rows_q = quarter(rep * 2 + target % 2)
        q = rep * 2 + target % 2
        mine = jnp.logical_and(tp == ad, ad == target)

        @pl.when(mine)
        def _():
            pltpu.make_async_copy(
                w_hbm.at[rows_q], weight.at[tp, rows_q], w_recv.at[tp, q]
            ).start()

        @pl.when(jnp.logical_not(mine))
        def _():
            remote(
                w_hbm.at[rows_q],
                weight.at[tp, rows_q],
                ws1.at[target],
                w_recv.at[tp, q],
                t=ad,
                a=target,
            ).start()

    seg_row = seg_ref[...]
    seg_col = jnp.transpose(
        jnp.broadcast_to(seg_row.astype(jnp.float32), (128, rows)), (1, 0)
    ).astype(jnp.int32)

    for d in range(1, 4):
        peer = lax.rem(ad + d, 4)
        remote(tenants.at[peer], tenants.at[peer], ten_send.at[peer], ten_recv.at[peer], a=peer).wait()
    to_smem = pltpu.make_async_copy(tenants, tenant_smem, local_sem.at[2])
    to_smem.start()
    to_smem.wait()
    load_down.wait()

    def picks(batch):
        chosen = [jnp.int32(0)] * SLOTS
        count = jnp.int32(0)
        for s in range(sequences):
            number = tenant_smem[batch, 0, s]
            here = number // held_count == ad
            for c in range(SLOTS):
                chosen[c] = jnp.where(
                    jnp.logical_and(here, count == c), lax.rem(number, held_count), chosen[c]
                )
            count = count + here.astype(jnp.int32)
        return chosen

    def fill(target_a, target_u, chosen, pair):
        for c in (2 * pair, 2 * pair + 1):
            target_a[pl.ds(c * rank, rank), :] = down[chosen[c]]
            target_u[pl.ds(c * rank, rank), :] = up_ref[chosen[c]]

    def half(ref, owner, pair):
        return ref.at[owner, pl.ds(pair * 2 * rank, 2 * rank)]

    picked = {}
    for pair in range(2):
        for name, peer in (("far0", far0), ("far1", far1)):
            if pair == 0:
                picked[name] = picks(peer)
            fill(send_a.at[peer], send_u.at[peer], picked[name], pair)
            remote(
                half(send_a, peer, pair),
                half(recv_a, ad, pair),
                a_send.at[peer, pair],
                a_recv.at[ad, pair],
                a=peer,
            ).start()
    picked["mate"] = picks(mate)
    for pair in range(2):
        fill(send_a.at[mate], send_u.at[mate], picked["mate"], pair)
        remote(
            half(send_a, mate, pair),
            half(recv_a, ad, pair),
            a_send.at[mate, pair],
            a_recv.at[ad, pair],
            a=mate,
        ).start()
    for peer in (far0, far1, mate):
        remote(
            send_u.at[peer], recv_u.at[ad], u_send.at[peer], u_recv.at[ad], a=peer
        ).start()

    q_own, q_mate = rep * 2 + core, rep * 2 + 1 - core
    y_own, y_mate = other_rep * 2 + core, other_rep * 2 + 1 - core

    def w_wait(t, q):
        remote(
            weight.at[t, quarter(q)], weight.at[t, quarter(q)], ws1.at[0], w_recv.at[t, q], a=mate
        ).wait_recv()

    def forward(t, q, k, to_rep):
        block = weight.at[t, quarter(q)]
        if to_rep:
            return remote(block, block, ws2.at[t, k], w_recv.at[t, q], r=other_rep)
        return remote(block, block, ws2.at[t, k], w_recv.at[t, q], a=mate)

    for d in range(4):
        t = lax.rem(tp + d, 4)
        w_wait(t, q_own)
        forward(t, q_own, 0, True).start()
        forward(t, q_own, 1, False).start()

    picked["own"] = picks(ad)
    for pair in range(2):
        fill(recv_a.at[ad], recv_u.at[ad], picked["own"], pair)

    for d in range(4):
        t = lax.rem(tp + d, 4)
        w_wait(t, y_own)
        forward(t, y_own, 2, False).start()

    firsts = jnp.sum(
        (
            jnp.broadcast_to(seg_row, (sequences, rows))
            < lax.broadcasted_iota(jnp.int32, (sequences, rows), 0)
        ).astype(jnp.float32),
        axis=1,
        keepdims=True,
    )
    first_angles = firsts * freq_ref[...]
    first_cos, first_sin = jnp.cos(first_angles), jnp.sin(first_angles)
    slots = jnp.zeros((rows, 128), jnp.int32)
    start_cos = jnp.zeros((rows, 128), jnp.float32)
    start_sin = jnp.zeros((rows, 128), jnp.float32)
    for s in range(sequences):
        owner = tenant_smem[ad, 0, s] // held_count
        before = jnp.int32(0)
        for e in range(s):
            before = before + (tenant_smem[ad, 0, e] // held_count == owner).astype(jnp.int32)
        hit = seg_col == s
        slots = jnp.where(hit, owner * SLOTS + before, slots)
        start_cos = jnp.where(hit, first_cos[s : s + 1], start_cos)
        start_sin = jnp.where(hit, first_sin[s : s + 1], start_sin)
    slot_col[...] = slots
    cosine[...] = cos_ref[...] * start_cos + sin_ref[...] * start_sin
    turn = sin_ref[...] * start_cos - cos_ref[...] * start_sin
    sine[...] = jnp.where(lane_half == 0, -turn, turn)
    shrink[...] = jnp.zeros_like(shrink)
    load_tok.wait()

    tile = 256
    NT = (((1,), (1,)), ((), ()))

    def base_product(t, target):
        @pl.loop(0, rows // tile)
        def _(m):
            at = pl.ds(pl.multiple_of(m * tile, tile), tile)
            product = jnp.dot(tok[at, :], weight[t], preferred_element_type=jnp.float32)
            target[at, :] = product.astype(target.dtype)

    def next_to(t):
        return jnp.logical_and(t < tp + 3, tp < t + 3)

    for d in (1, 2, 3, 0):
        t = lax.rem(tp + d, 4)
        w_wait(t, q_mate)
        w_wait(t, y_mate)
        if d:

            @pl.when(next_to(t))
            def _():
                base_product(t, wide_send.at[t])
                remote(wide_send.at[t], wide_recv.at[tp], p_send.at[t], p_recv.at[tp], t=t).start()

            @pl.when(jnp.logical_not(next_to(t)))
            def _():
                base_product(t, part_send.at[t])
                remote(part_send.at[t], part_recv.at[tp], p_send.at[t], p_recv.at[tp], t=t).start()

        else:
            base_product(t, part_own)

    def shrink_product(owner, pair):
        @pl.loop(0, rows // tile)
        def _(m):
            at = pl.ds(pl.multiple_of(m * tile, tile), tile)
            product = lax.dot_general(
                tok[at, :],
                recv_a[owner, pl.ds(pair * 2 * rank, 2 * rank), :],
                NT,
                preferred_element_type=jnp.float32,
            )
            wanted = owner * SLOTS + pair * 2 + lane_half[:tile]
            shrink[at, :] = jnp.where(slot_col[at, :] == wanted, product, shrink[at, :])

    def a_wait(owner, pair):
        remote(
            half(recv_a, owner, pair),
            half(recv_a, owner, pair),
            a_send.at[owner, pair],
            a_recv.at[owner, pair],
            a=owner,
        ).wait_recv()

    for pair in range(2):
        shrink_product(ad, pair)
    for pair in range(2):
        a_wait(mate, pair)
        shrink_product(mate, pair)
    kv_index = tp // (4 // key_ref.shape[1])
    for source, chosen in ((key_ref, key_head), (value_ref, value_head)):

        @pl.loop(0, rows // 128)
        def _(m):
            at = pl.ds(pl.multiple_of(m * 128, 128), 128)
            block = source[at].astype(jnp.float32)
            kept = lax.broadcasted_iota(jnp.int32, block.shape, 1) == kv_index
            chosen[at, :] = jnp.sum(jnp.where(kept, block, 0.0), axis=1).astype(jnp.bfloat16)

    for pair in range(2):
        for owner in (far0, far1):
            a_wait(owner, pair)
            shrink_product(owner, pair)

    both = shrink[...] + pltpu.roll(shrink[...], rank, 1)
    low = rows // 2
    packed[...] = jnp.where(lane_half[:low] == 0, both[:low], both[low:])
    span = low // 4

    def piece(t):
        return pl.ds(pl.multiple_of(t * span, span), span)

    for d in range(1, 4):
        t = lax.rem(tp + d, 4)
        remote(packed.at[piece(t)], quarter_recv.at[tp], q_send.at[t], q_recv.at[tp], t=t).start()
    quarter_recv[tp] = packed[piece(tp), :]
    for d in range(1, 4):
        t = lax.rem(tp + d, 4)
        remote(packed.at[piece(t)], quarter_recv.at[t], q_send.at[t], q_recv.at[t], t=t).wait_recv()
    total = (quarter_recv[0] + quarter_recv[1]) + (quarter_recv[2] + quarter_recv[3])
    rounded[tp] = total.astype(jnp.bfloat16)
    for d in range(1, 4):
        t = lax.rem(tp + d, 4)
        remote(rounded.at[tp], rounded.at[tp], g_send.at[t], g_recv.at[tp], t=t).start()

    for d in range(1, 4):
        t = lax.rem(tp + d, 4)

        @pl.when(next_to(t))
        def _():
            remote(wide_send.at[t], wide_recv.at[t], p_send.at[t], p_recv.at[t], t=t).wait()
            part_own[...] += wide_recv[t]

        @pl.when(jnp.logical_not(next_to(t)))
        def _():
            remote(part_send.at[t], part_recv.at[t], p_send.at[t], p_recv.at[t], t=t).wait()
            part_own[...] += part_recv[t].astype(jnp.float32)

        peer = lax.rem(ad + d, 4)
        remote(send_u.at[peer], recv_u.at[peer], u_send.at[peer], u_recv.at[peer], a=peer).wait()
        remote(packed.at[piece(t)], quarter_recv.at[t], q_send.at[t], q_recv.at[t], t=t).wait_send()
        for pair in range(2):
            remote(
                half(send_a, peer, pair),
                half(recv_a, peer, pair),
                a_send.at[peer, pair],
                a_recv.at[peer, pair],
                a=peer,
            ).wait_send()
    for d in range(4):
        forward(d, q_own, 0, True).wait_send()
        forward(d, q_own, 1, False).wait_send()
        forward(d, y_own, 2, False).wait_send()
    for target in range(4):
        rows_q = quarter(rep * 2 + target % 2)
        mine = jnp.logical_and(tp == ad, ad == target)

        @pl.when(jnp.logical_not(mine))
        def _():
            remote(
                w_hbm.at[rows_q],
                weight.at[tp, rows_q],
                ws1.at[target],
                w_recv.at[tp, rep * 2 + target % 2],
                t=ad,
                a=target,
            ).wait_send()

    for d in range(1, 4):
        t = lax.rem(tp + d, 4)
        remote(rounded.at[t], rounded.at[t], g_send.at[t], g_recv.at[t], t=t).wait()

    scale = 1.0 / math.sqrt(head)
    half_low = lane_half[:span]
    top, bottom = [], []
    for t in range(4):
        values = rounded[t].astype(jnp.float32)
        turned = pltpu.roll(values, rank, 1)
        top.append(jnp.where(half_low == 0, values, turned))
        bottom.append(jnp.where(half_low == 0, turned, values))
    shrink[...] = jnp.concatenate(top + bottom, axis=0)

    for start in range(0, rows, tile):
        at = pl.ds(start, tile)
        slots_here = slot_col[at, :]
        shrink_here = shrink[at, :]
        adapted = jnp.zeros((tile, head), jnp.float32)
        for owner in range(4):
            for pair in range(2):
                wanted = owner * SLOTS + pair * 2 + lane_half[:tile]
                spread = jnp.where(slots_here == wanted, shrink_here, 0.0).astype(jnp.bfloat16)
                adapted = adapted + jnp.dot(
                    spread,
                    recv_u[owner, pl.ds(pair * 2 * rank, 2 * rank), :],
                    preferred_element_type=jnp.float32,
                )
        combined = part_own[at, :] + adapter_scale * adapted
        queries = (
            combined * cosine[at, :] + pltpu.roll(combined, head // 2, 1) * sine[at, :]
        ).astype(jnp.bfloat16)
        first = max(0, start - tile)
        width = start + tile - first
        scores = (
            lax.dot_general(
                queries, key_head[pl.ds(first, width), :], NT, preferred_element_type=jnp.float32
            )
            * scale
        )
        row_at = start + lax.broadcasted_iota(jnp.int32, (tile, width), 0)
        col_at = first + lax.broadcasted_iota(jnp.int32, (tile, width), 1)
        row_seg = jnp.transpose(
            jnp.broadcast_to(seg_row[:, start : start + tile].astype(jnp.float32), (128, tile)),
            (1, 0),
        )[:, :1].astype(jnp.int32)
        allowed = jnp.logical_and(row_seg == seg_row[:, first : first + width], col_at <= row_at)
        masked = jnp.where(allowed, scores, -jnp.inf)
        highest = jnp.max(masked, axis=1, keepdims=True)
        expanded = jnp.where(allowed, jnp.exp(scores - highest), 0.0)
        probs = (expanded / jnp.sum(expanded, axis=1, keepdims=True)).astype(jnp.bfloat16)
        out_ref[at, :] = jnp.dot(
            probs, value_head[pl.ds(first, width), :], preferred_element_type=jnp.float32
        ).astype(jnp.bfloat16)


def fused_body(
    tokens,
    query_base_weight,
    adapter_down_weight,
    adapter_up_weight,
    rotated_key_cache,
    value_cache_rows,
    segment_index,
    tenant_index,
):
    rows, depth = tokens.shape
    held, _, rank = adapter_down_weight.shape
    head = query_base_weight.shape[1]
    exponent = np.arange(head // 2, dtype=np.float32) * np.float32(2.0 / head)
    frequency = np.power(np.float32(rope_theta), -exponent).astype(np.float32)
    freq_row = jnp.asarray(np.concatenate([frequency, frequency])[None, :])
    both = np.concatenate([frequency, frequency]).astype(np.float64)
    table = np.arange(rows, dtype=np.float64)[:, None] * both[None, :]
    bf16, f32 = jnp.bfloat16, jnp.float32
    DMA = pltpu.SemaphoreType.DMA
    vmem = pl.BlockSpec(memory_space=pltpu.VMEM)
    anywhere = pl.BlockSpec(memory_space=pl.ANY)
    return pl.pallas_call(
        fused_kernel,
        out_shape=jax.ShapeDtypeStruct((rows, head), bf16),
        in_specs=[anywhere] * 3 + [vmem] * 8,
        out_specs=vmem,
        scratch_shapes=[
            pltpu.VMEM((rows, depth), bf16),
            pltpu.VMEM((held, rank, depth), bf16),
            pltpu.VMEM((4, depth, head), bf16),
            pltpu.VMEM((4, SLOTS * rank, depth), bf16),
            pltpu.VMEM((4, SLOTS * rank, depth), bf16),
            pltpu.VMEM((4, SLOTS * rank, head), bf16),
            pltpu.VMEM((4, SLOTS * rank, head), bf16),
            pltpu.VMEM((4, 8, 128), jnp.int32),
            pltpu.SMEM((4, 8, 128), jnp.int32),
            pltpu.VMEM((4, rows, head), bf16),
            pltpu.VMEM((4, rows, head), bf16),
            pltpu.VMEM((rows, head), f32),
            pltpu.VMEM((4, rows, head), f32),
            pltpu.VMEM((4, rows, head), f32),
            pltpu.VMEM((rows, 128), jnp.int32),
            pltpu.VMEM((rows, 128), f32),
            pltpu.VMEM((rows, 128), f32),
            pltpu.VMEM((rows, 128), f32),
            pltpu.VMEM((rows // 2, 128), f32),
            pltpu.VMEM((4, rows // 8, 128), f32),
            pltpu.VMEM((4, rows // 8, 128), bf16),
            pltpu.VMEM((rows, head), bf16),
            pltpu.VMEM((rows, head), bf16),
            DMA((3,)),
            DMA((4,)),
            DMA((4,)),
            DMA((4,)),
            DMA((4, 3)),
            DMA((4, 4)),
            DMA((4, 2)),
            DMA((4, 2)),
            DMA((4,)),
            DMA((4,)),
            DMA((4,)),
            DMA((4,)),
            DMA((4,)),
            DMA((4,)),
            DMA((4,)),
            DMA((4,)),
        ],
        compiler_params=pltpu.CompilerParams(
            collective_id=0, has_side_effects=True, vmem_limit_bytes=56 * 1024 * 1024
        ),
        cost_estimate=pl.CostEstimate(
            flops=2 * rows * depth * 12 * head, bytes_accessed=20 << 20, transcendentals=1 << 20
        ),
    )(
        tokens,
        query_base_weight,
        jnp.transpose(adapter_down_weight, (0, 2, 1)),
        adapter_up_weight,
        rotated_key_cache,
        value_cache_rows,
        segment_index,
        tenant_index,
        freq_row,
        jnp.asarray(np.cos(table).astype(np.float32)),
        jnp.asarray(np.sin(table).astype(np.float32)),
    )


def solution(mesh):
    square = dict(mesh.shape) == {"rep": 2, "tp": 4, "ad": 4}
    return jax.shard_map(
        fused_body if square else body,
        mesh=mesh,
        in_specs=(
            P(("rep", "ad"), "tp"),
            P("ad", "tp"),
            P("ad", "tp", None),
            P("ad", None, "tp"),
            P(("rep", "ad"), None, None),
            P(("rep", "ad"), None, None),
            P(("rep", "ad"), None),
            P(("rep", "ad"), None),
        ),
        out_specs=P(("rep", "ad"), "tp"),
        check_vma=False,
    )
```

```python
import math

import jax
import jax.numpy as jnp
import numpy as np
from jax import lax
from jax.experimental import pallas as pl
from jax.experimental.pallas import tpu as pltpu
from jax.sharding import PartitionSpec as P

rope_theta = 500000.0
adapter_scale = 0.5
SLOTS = 4
MESH = pl.DeviceIdType.MESH


def positions_of(segment_row):
    length = segment_row.shape[0]
    indices = jnp.arange(length, dtype=jnp.int32)
    starting = jnp.concatenate([jnp.ones((1,), jnp.bool_), segment_row[1:] != segment_row[:-1]])
    earliest = lax.cummax(jnp.where(starting, indices, jnp.zeros_like(indices)), axis=0)
    return (indices - earliest).astype(jnp.float32)


def rotate(matrix, position):
    half_width = matrix.shape[-1] // 2
    exponent = jnp.arange(half_width, dtype=jnp.float32) * (2.0 / matrix.shape[-1])
    frequency = jnp.power(jnp.float32(rope_theta), -exponent)
    angles = position[:, None] * frequency[None, :]
    cosine = jnp.cos(angles)
    sine = jnp.sin(angles)
    leading = matrix[..., :half_width]
    trailing = matrix[..., half_width:]
    return jnp.concatenate(
        [leading * cosine - trailing * sine, trailing * cosine + leading * sine], axis=-1
    )


def attend(query_head, key_head, value_head, segment_row):
    length = segment_row.shape[0]
    indices = jnp.arange(length, dtype=jnp.int32)
    scores = jnp.dot(query_head, key_head.T, preferred_element_type=jnp.float32) * (
        1.0 / jnp.sqrt(jnp.float32(query_head.shape[-1]))
    )
    allowed = (segment_row[:, None] == segment_row[None, :]) & (
        indices[None, :] <= indices[:, None]
    )
    masked = jnp.where(allowed, scores, -jnp.inf)
    highest = jnp.max(masked, axis=1, keepdims=True)
    expanded = jnp.where(allowed, jnp.exp(scores - highest), jnp.float32(0.0))
    totals = jnp.sum(expanded, axis=1, keepdims=True)
    probs = (expanded / totals).astype(jnp.bfloat16)
    return jnp.dot(probs, value_head, preferred_element_type=jnp.float32).astype(jnp.bfloat16)


def body(
    tokens,
    query_base_weight,
    adapter_down_weight,
    adapter_up_weight,
    rotated_key_cache,
    value_cache_rows,
    segment_index,
    tenant_index,
):
    segment_row = segment_index[0]
    token_tenants = tenant_index[0]
    sequences = token_tenants.shape[0]
    row_count = tokens.shape[0]
    adapter_rank_width = adapter_down_weight.shape[2]
    head_width = query_base_weight.shape[1]
    feature_matrix = adapter_down_weight.shape[1]
    onehot = segment_row[:, None] == jnp.arange(sequences, dtype=jnp.int32)[None, :]
    gathered = lax.all_gather(tokens, "tp", axis=1, tiled=True)
    base_output = jnp.dot(
        gathered,
        lax.all_gather(query_base_weight, "ad", axis=0, tiled=True),
        preferred_element_type=jnp.float32,
    )
    portions = (
        lax.all_gather(adapter_down_weight, "ad", axis=0, tiled=True),
        lax.all_gather(adapter_up_weight, "ad", axis=0, tiled=True),
    )
    count = portions[0].shape[0]
    lookup = (token_tenants[:, None] == jnp.arange(count, dtype=jnp.int32)[None, :]).astype(
        jnp.bfloat16
    )
    down_part = jnp.einsum("sn,nxr->sxr", lookup, portions[0], preferred_element_type=jnp.float32)
    up_part = jnp.einsum("sn,nrh->srh", lookup, portions[1], preferred_element_type=jnp.float32)
    selected_down = down_part.astype(jnp.bfloat16)
    up_sel = up_part.astype(jnp.bfloat16)
    selected_down, up_sel = (selected_down, up_sel)
    down_flat = jnp.transpose(selected_down, (1, 0, 2)).reshape(
        feature_matrix, sequences * adapter_rank_width
    )
    partial_all = jnp.dot(tokens, down_flat, preferred_element_type=jnp.float32).reshape(
        row_count, sequences, adapter_rank_width
    )
    partial_sum = jnp.sum(jnp.where(onehot[:, :, None], partial_all, jnp.float32(0.0)), axis=1)
    shrink_b = lax.psum(partial_sum, "tp").astype(jnp.bfloat16)
    spread = jnp.where(onehot[:, :, None], shrink_b[:, None, :], jnp.zeros((), jnp.bfloat16))
    flat_rows = spread.reshape(row_count, sequences * adapter_rank_width)
    adapted_queries = jnp.dot(
        flat_rows,
        up_sel.reshape(sequences * adapter_rank_width, head_width),
        preferred_element_type=jnp.float32,
    )
    combined_queries = base_output + adapter_scale * adapted_queries
    queries = rotate(combined_queries, positions_of(segment_row)).astype(jnp.bfloat16)
    heads_total = lax.axis_size("tp")
    kv_heads = rotated_key_cache.shape[1]
    kv_index = lax.axis_index("tp") // (heads_total // kv_heads)
    key_head = lax.dynamic_index_in_dim(rotated_key_cache, kv_index, 1, keepdims=False)
    value_head = lax.dynamic_index_in_dim(value_cache_rows, kv_index, 1, keepdims=False)
    return attend(queries, key_head, value_head, segment_row)


def fused_kernel(
    tok_hbm,
    w_hbm,
    down_hbm,
    up_ref,
    key_ref,
    value_ref,
    seg_ref,
    tenant_ref,
    freq_ref,
    cos_ref,
    sin_ref,
    out_ref,
    tok,
    down,
    weight,
    send_a,
    recv_a,
    send_u,
    recv_u,
    tenants,
    tenant_smem,
    part_send,
    part_recv,
    part_own,
    wide_send,
    wide_recv,
    slot_col,
    cosine,
    sine,
    shrink,
    packed,
    quarter_recv,
    rounded,
    key_head,
    value_head,
    local_sem,
    ten_send,
    ten_recv,
    ws1,
    ws2,
    w_recv,
    a_send,
    a_recv,
    u_send,
    u_recv,
    p_send,
    p_recv,
    q_send,
    q_recv,
    g_send,
    g_recv,
):
    rep, tp, ad = lax.axis_index("rep"), lax.axis_index("tp"), lax.axis_index("ad")
    rows, depth = tok.shape
    rank = down.shape[1]
    held_count = down.shape[0]
    head = weight.shape[2]
    sequences = SLOTS * 2
    core = lax.rem(ad, 2)
    mate = ad + 1 - 2 * core
    far0 = lax.rem(ad + 2, 4)
    far1 = far0 + 1 - 2 * lax.rem(far0, 2)
    other_rep = 1 - rep
    lane = lax.broadcasted_iota(jnp.int32, (rows, 128), 1)
    lane_half = lane // rank

    def remote(src, dst, ss, rs, r=None, t=None, a=None):
        return pltpu.make_async_remote_copy(
            src_ref=src,
            dst_ref=dst,
            send_sem=ss,
            recv_sem=rs,
            device_id=(rep if r is None else r, tp if t is None else t, ad if a is None else a),
            device_id_type=MESH,
        )

    load_down = pltpu.make_async_copy(down_hbm, down, local_sem.at[0])
    load_tok = pltpu.make_async_copy(tok_hbm, tok, local_sem.at[1])
    load_down.start()
    load_tok.start()

    barrier = pltpu.get_barrier_semaphore()
    for dt in range(4):
        for da in range(4):
            if dt or da:
                pl.semaphore_signal(
                    barrier,
                    inc=1,
                    device_id=(rep, lax.rem(tp + dt, 4), lax.rem(ad + da, 4)),
                    device_id_type=MESH,
                )
    pl.semaphore_signal(barrier, inc=1, device_id=(other_rep, tp, ad), device_id_type=MESH)
    pl.semaphore_wait(barrier, 16)

    tenants[ad] = jnp.zeros(tenants.shape[1:], jnp.int32)
    tenants[ad, 0:1, 0 : tenant_ref.shape[1]] = tenant_ref[...]
    for d in range(1, 4):
        peer = lax.rem(ad + d, 4)
        remote(tenants.at[ad], tenants.at[ad], ten_send.at[peer], ten_recv.at[ad], a=peer).start()

    part = depth // 4

    def quarter(q):
        return pl.ds(pl.multiple_of(q * part, part), part)

    for target in range(4):
        rows_q = quarter(rep * 2 + target % 2)
        q = rep * 2 + target % 2
        mine = jnp.logical_and(tp == ad, ad == target)

        @pl.when(mine)
        def _():
            pltpu.make_async_copy(
                w_hbm.at[rows_q], weight.at[tp, rows_q], w_recv.at[tp, q]
            ).start()

        @pl.when(jnp.logical_not(mine))
        def _():
            remote(
                w_hbm.at[rows_q],
                weight.at[tp, rows_q],
                ws1.at[target],
                w_recv.at[tp, q],
                t=ad,
                a=target,
            ).start()

    seg_row = seg_ref[...]
    seg_col = jnp.transpose(
        jnp.broadcast_to(seg_row.astype(jnp.float32), (128, rows)), (1, 0)
    ).astype(jnp.int32)

    for d in range(1, 4):
        peer = lax.rem(ad + d, 4)
        remote(tenants.at[peer], tenants.at[peer], ten_send.at[peer], ten_recv.at[peer], a=peer).wait()
    to_smem = pltpu.make_async_copy(tenants, tenant_smem, local_sem.at[2])
    to_smem.start()
    to_smem.wait()
    load_down.wait()

    def picks(batch):
        chosen = [jnp.int32(0)] * SLOTS
        count = jnp.int32(0)
        for s in range(sequences):
            number = tenant_smem[batch, 0, s]
            here = number // held_count == ad
            for c in range(SLOTS):
                chosen[c] = jnp.where(
                    jnp.logical_and(here, count == c), lax.rem(number, held_count), chosen[c]
                )
            count = count + here.astype(jnp.int32)
        return chosen

    def fill(target_a, target_u, chosen, pair):
        for c in (2 * pair, 2 * pair + 1):
            target_a[pl.ds(c * rank, rank), :] = down[chosen[c]]
            target_u[pl.ds(c * rank, rank), :] = up_ref[chosen[c]]

    def half(ref, owner, pair):
        return ref.at[owner, pl.ds(pair * 2 * rank, 2 * rank)]

    picked = {}
    for pair in range(2):
        for name, peer in (("far0", far0), ("far1", far1)):
            if pair == 0:
                picked[name] = picks(peer)
            fill(send_a.at[peer], send_u.at[peer], picked[name], pair)
            remote(
                half(send_a, peer, pair),
                half(recv_a, ad, pair),
                a_send.at[peer, pair],
                a_recv.at[ad, pair],
                a=peer,
            ).start()
    picked["mate"] = picks(mate)
    for pair in range(2):
        fill(send_a.at[mate], send_u.at[mate], picked["mate"], pair)
        remote(
            half(send_a, mate, pair),
            half(recv_a, ad, pair),
            a_send.at[mate, pair],
            a_recv.at[ad, pair],
            a=mate,
        ).start()
    for peer in (far0, far1, mate):
        remote(
            send_u.at[peer], recv_u.at[ad], u_send.at[peer], u_recv.at[ad], a=peer
        ).start()

    q_own, q_mate = rep * 2 + core, rep * 2 + 1 - core
    y_own, y_mate = other_rep * 2 + core, other_rep * 2 + 1 - core

    def w_wait(t, q):
        remote(
            weight.at[t, quarter(q)], weight.at[t, quarter(q)], ws1.at[0], w_recv.at[t, q], a=mate
        ).wait_recv()

    def forward(t, q, k, to_rep):
        block = weight.at[t, quarter(q)]
        if to_rep:
            return remote(block, block, ws2.at[t, k], w_recv.at[t, q], r=other_rep)
        return remote(block, block, ws2.at[t, k], w_recv.at[t, q], a=mate)

    for d in range(4):
        t = lax.rem(tp + d, 4)
        w_wait(t, q_own)
        forward(t, q_own, 0, True).start()
        forward(t, q_own, 1, False).start()

    picked["own"] = picks(ad)
    for pair in range(2):
        fill(recv_a.at[ad], recv_u.at[ad], picked["own"], pair)

    for d in range(4):
        t = lax.rem(tp + d, 4)
        w_wait(t, y_own)
        forward(t, y_own, 2, False).start()

    firsts = jnp.sum(
        (
            jnp.broadcast_to(seg_row, (sequences, rows))
            < lax.broadcasted_iota(jnp.int32, (sequences, rows), 0)
        ).astype(jnp.float32),
        axis=1,
        keepdims=True,
    )
    first_angles = firsts * freq_ref[...]
    first_cos, first_sin = jnp.cos(first_angles), jnp.sin(first_angles)
    slots = jnp.zeros((rows, 128), jnp.int32)
    start_cos = jnp.zeros((rows, 128), jnp.float32)
    start_sin = jnp.zeros((rows, 128), jnp.float32)
    for s in range(sequences):
        owner = tenant_smem[ad, 0, s] // held_count
        before = jnp.int32(0)
        for e in range(s):
            before = before + (tenant_smem[ad, 0, e] // held_count == owner).astype(jnp.int32)
        hit = seg_col == s
        slots = jnp.where(hit, owner * SLOTS + before, slots)
        start_cos = jnp.where(hit, first_cos[s : s + 1], start_cos)
        start_sin = jnp.where(hit, first_sin[s : s + 1], start_sin)
    slot_col[...] = slots
    cosine[...] = cos_ref[...] * start_cos + sin_ref[...] * start_sin
    turn = sin_ref[...] * start_cos - cos_ref[...] * start_sin
    sine[...] = jnp.where(lane_half == 0, -turn, turn)
    shrink[...] = jnp.zeros_like(shrink)
    load_tok.wait()

    tile = 256
    NT = (((1,), (1,)), ((), ()))

    def base_product(t, target):
        @pl.loop(0, rows // tile)
        def _(m):
            at = pl.ds(pl.multiple_of(m * tile, tile), tile)
            product = jnp.dot(tok[at, :], weight[t], preferred_element_type=jnp.float32)
            target[at, :] = product.astype(target.dtype)

    def next_to(t):
        return jnp.logical_or(t == tp + 1, t + 1 == tp)

    for d in (1, 2, 3, 0):
        t = lax.rem(tp + d, 4)
        w_wait(t, q_mate)
        w_wait(t, y_mate)
        if d:

            @pl.when(next_to(t))
            def _():
                base_product(t, wide_send.at[t])
                remote(wide_send.at[t], wide_recv.at[tp], p_send.at[t], p_recv.at[tp], t=t).start()

            @pl.when(jnp.logical_not(next_to(t)))
            def _():
                base_product(t, part_send.at[t])
                remote(part_send.at[t], part_recv.at[tp], p_send.at[t], p_recv.at[tp], t=t).start()

        else:
            base_product(t, part_own)

    def shrink_product(owner):
        @pl.loop(0, rows // tile)
        def _(m):
            at = pl.ds(pl.multiple_of(m * tile, tile), tile)
            product = lax.dot_general(
                tok[at, :], recv_a[owner], NT, preferred_element_type=jnp.float32
            )
            kept = shrink[at, :]
            for pair in range(2):
                wanted = owner * SLOTS + pair * 2 + lane_half[:tile]
                kept = jnp.where(
                    slot_col[at, :] == wanted, product[:, pair * 128 : pair * 128 + 128], kept
                )
            shrink[at, :] = kept

    def a_wait(owner, pair):
        remote(
            half(recv_a, owner, pair),
            half(recv_a, owner, pair),
            a_send.at[owner, pair],
            a_recv.at[owner, pair],
            a=owner,
        ).wait_recv()

    shrink_product(ad)
    for pair in range(2):
        a_wait(mate, pair)
    shrink_product(mate)
    kv_index = tp // (4 // key_ref.shape[1])
    for source, chosen in ((key_ref, key_head), (value_ref, value_head)):

        @pl.loop(0, rows // 128)
        def _(m):
            at = pl.ds(pl.multiple_of(m * 128, 128), 128)
            block = source[at].astype(jnp.float32)
            kept = lax.broadcasted_iota(jnp.int32, block.shape, 1) == kv_index
            chosen[at, :] = jnp.sum(jnp.where(kept, block, 0.0), axis=1).astype(jnp.bfloat16)

    for owner in (far0, far1):
        for pair in range(2):
            a_wait(owner, pair)
        shrink_product(owner)

    both = shrink[...] + pltpu.roll(shrink[...], rank, 1)
    low = rows // 2
    packed[...] = jnp.where(lane_half[:low] == 0, both[:low], both[low:])
    span = low // 4

    def piece(t):
        return pl.ds(pl.multiple_of(t * span, span), span)

    for d in range(1, 4):
        t = lax.rem(tp + d, 4)
        remote(packed.at[piece(t)], quarter_recv.at[tp], q_send.at[t], q_recv.at[tp], t=t).start()
    quarter_recv[tp] = packed[piece(tp), :]
    for d in range(1, 4):
        t = lax.rem(tp + d, 4)
        remote(packed.at[piece(t)], quarter_recv.at[t], q_send.at[t], q_recv.at[t], t=t).wait_recv()
    total = (quarter_recv[0] + quarter_recv[1]) + (quarter_recv[2] + quarter_recv[3])
    rounded[tp] = total.astype(jnp.bfloat16)
    for d in range(1, 4):
        t = lax.rem(tp + d, 4)
        remote(rounded.at[tp], rounded.at[tp], g_send.at[t], g_recv.at[tp], t=t).start()

    for d in range(1, 4):
        t = lax.rem(tp + d, 4)

        @pl.when(next_to(t))
        def _():
            remote(wide_send.at[t], wide_recv.at[t], p_send.at[t], p_recv.at[t], t=t).wait()
            part_own[...] += wide_recv[t]

        @pl.when(jnp.logical_not(next_to(t)))
        def _():
            remote(part_send.at[t], part_recv.at[t], p_send.at[t], p_recv.at[t], t=t).wait()
            part_own[...] += part_recv[t].astype(jnp.float32)

        peer = lax.rem(ad + d, 4)
        remote(send_u.at[peer], recv_u.at[peer], u_send.at[peer], u_recv.at[peer], a=peer).wait()
        remote(packed.at[piece(t)], quarter_recv.at[t], q_send.at[t], q_recv.at[t], t=t).wait_send()
        for pair in range(2):
            remote(
                half(send_a, peer, pair),
                half(recv_a, peer, pair),
                a_send.at[peer, pair],
                a_recv.at[peer, pair],
                a=peer,
            ).wait_send()
    for d in range(4):
        forward(d, q_own, 0, True).wait_send()
        forward(d, q_own, 1, False).wait_send()
        forward(d, y_own, 2, False).wait_send()
    for target in range(4):
        rows_q = quarter(rep * 2 + target % 2)
        mine = jnp.logical_and(tp == ad, ad == target)

        @pl.when(jnp.logical_not(mine))
        def _():
            remote(
                w_hbm.at[rows_q],
                weight.at[tp, rows_q],
                ws1.at[target],
                w_recv.at[tp, rep * 2 + target % 2],
                t=ad,
                a=target,
            ).wait_send()

    for d in range(1, 4):
        t = lax.rem(tp + d, 4)
        remote(rounded.at[t], rounded.at[t], g_send.at[t], g_recv.at[t], t=t).wait()

    scale = 1.0 / math.sqrt(head)
    half_low = lane_half[:span]
    top, bottom = [], []
    for t in range(4):
        values = rounded[t].astype(jnp.float32)
        turned = pltpu.roll(values, rank, 1)
        top.append(jnp.where(half_low == 0, values, turned))
        bottom.append(jnp.where(half_low == 0, turned, values))
    shrink[...] = jnp.concatenate(top + bottom, axis=0)

    for start in range(0, rows, tile):
        at = pl.ds(start, tile)
        slots_here = slot_col[at, :]
        shrink_here = shrink[at, :]
        adapted = jnp.zeros((tile, head), jnp.float32)
        for owner in range(4):
            for pair in range(2):
                wanted = owner * SLOTS + pair * 2 + lane_half[:tile]
                spread = jnp.where(slots_here == wanted, shrink_here, 0.0).astype(jnp.bfloat16)
                adapted = adapted + jnp.dot(
                    spread,
                    recv_u[owner, pl.ds(pair * 2 * rank, 2 * rank), :],
                    preferred_element_type=jnp.float32,
                )
        combined = part_own[at, :] + adapter_scale * adapted
        queries = (
            combined * cosine[at, :] + pltpu.roll(combined, head // 2, 1) * sine[at, :]
        ).astype(jnp.bfloat16)
        first = max(0, start - tile)
        width = start + tile - first
        scores = (
            lax.dot_general(
                queries, key_head[pl.ds(first, width), :], NT, preferred_element_type=jnp.float32
            )
            * scale
        )
        row_at = start + lax.broadcasted_iota(jnp.int32, (tile, width), 0)
        col_at = first + lax.broadcasted_iota(jnp.int32, (tile, width), 1)
        row_seg = jnp.transpose(
            jnp.broadcast_to(seg_row[:, start : start + tile].astype(jnp.float32), (128, tile)),
            (1, 0),
        )[:, :1].astype(jnp.int32)
        allowed = jnp.logical_and(row_seg == seg_row[:, first : first + width], col_at <= row_at)
        masked = jnp.where(allowed, scores, -jnp.inf)
        highest = jnp.max(masked, axis=1, keepdims=True)
        expanded = jnp.where(allowed, jnp.exp(scores - highest), 0.0)
        probs = (expanded / jnp.sum(expanded, axis=1, keepdims=True)).astype(jnp.bfloat16)
        out_ref[at, :] = jnp.dot(
            probs, value_head[pl.ds(first, width), :], preferred_element_type=jnp.float32
        ).astype(jnp.bfloat16)


def fused_body(
    tokens,
    query_base_weight,
    adapter_down_weight,
    adapter_up_weight,
    rotated_key_cache,
    value_cache_rows,
    segment_index,
    tenant_index,
):
    rows, depth = tokens.shape
    held, _, rank = adapter_down_weight.shape
    head = query_base_weight.shape[1]
    exponent = np.arange(head // 2, dtype=np.float32) * np.float32(2.0 / head)
    frequency = np.power(np.float32(rope_theta), -exponent).astype(np.float32)
    freq_row = jnp.asarray(np.concatenate([frequency, frequency])[None, :])
    both = np.concatenate([frequency, frequency]).astype(np.float64)
    table = np.arange(rows, dtype=np.float64)[:, None] * both[None, :]
    bf16, f32 = jnp.bfloat16, jnp.float32
    DMA = pltpu.SemaphoreType.DMA
    vmem = pl.BlockSpec(memory_space=pltpu.VMEM)
    anywhere = pl.BlockSpec(memory_space=pl.ANY)
    return pl.pallas_call(
        fused_kernel,
        out_shape=jax.ShapeDtypeStruct((rows, head), bf16),
        in_specs=[anywhere] * 3 + [vmem] * 8,
        out_specs=vmem,
        scratch_shapes=[
            pltpu.VMEM((rows, depth), bf16),
            pltpu.VMEM((held, rank, depth), bf16),
            pltpu.VMEM((4, depth, head), bf16),
            pltpu.VMEM((4, SLOTS * rank, depth), bf16),
            pltpu.VMEM((4, SLOTS * rank, depth), bf16),
            pltpu.VMEM((4, SLOTS * rank, head), bf16),
            pltpu.VMEM((4, SLOTS * rank, head), bf16),
            pltpu.VMEM((4, 8, 128), jnp.int32),
            pltpu.SMEM((4, 8, 128), jnp.int32),
            pltpu.VMEM((4, rows, head), bf16),
            pltpu.VMEM((4, rows, head), bf16),
            pltpu.VMEM((rows, head), f32),
            pltpu.VMEM((4, rows, head), f32),
            pltpu.VMEM((4, rows, head), f32),
            pltpu.VMEM((rows, 128), jnp.int32),
            pltpu.VMEM((rows, 128), f32),
            pltpu.VMEM((rows, 128), f32),
            pltpu.VMEM((rows, 128), f32),
            pltpu.VMEM((rows // 2, 128), f32),
            pltpu.VMEM((4, rows // 8, 128), f32),
            pltpu.VMEM((4, rows // 8, 128), bf16),
            pltpu.VMEM((rows, head), bf16),
            pltpu.VMEM((rows, head), bf16),
            DMA((3,)),
            DMA((4,)),
            DMA((4,)),
            DMA((4,)),
            DMA((4, 3)),
            DMA((4, 4)),
            DMA((4, 2)),
            DMA((4, 2)),
            DMA((4,)),
            DMA((4,)),
            DMA((4,)),
            DMA((4,)),
            DMA((4,)),
            DMA((4,)),
            DMA((4,)),
            DMA((4,)),
        ],
        compiler_params=pltpu.CompilerParams(
            collective_id=0, has_side_effects=True, vmem_limit_bytes=56 * 1024 * 1024
        ),
        cost_estimate=pl.CostEstimate(
            flops=2 * rows * depth * 12 * head, bytes_accessed=20 << 20, transcendentals=1 << 20
        ),
    )(
        tokens,
        query_base_weight,
        jnp.transpose(adapter_down_weight, (0, 2, 1)),
        adapter_up_weight,
        rotated_key_cache,
        value_cache_rows,
        segment_index,
        tenant_index,
        freq_row,
        jnp.asarray(np.cos(table).astype(np.float32)),
        jnp.asarray(np.sin(table).astype(np.float32)),
    )


def solution(mesh):
    square = dict(mesh.shape) == {"rep": 2, "tp": 4, "ad": 4}
    return jax.shard_map(
        fused_body if square else body,
        mesh=mesh,
        in_specs=(
            P(("rep", "ad"), "tp"),
            P("ad", "tp"),
            P("ad", "tp", None),
            P("ad", None, "tp"),
            P(("rep", "ad"), None, None),
            P(("rep", "ad"), None, None),
            P(("rep", "ad"), None),
            P(("rep", "ad"), None),
        ),
        out_specs=P(("rep", "ad"), "tp"),
        check_vma=False,
    )
```
